32 devices in a mesh: row: 4 (over z), rep: 4 (over y, x), feat: 2 (over core).
Axes of the slice: x: 2, y: 2, z: 4, core: 2. Of those that a mesh axis runs over, the one named last changes fastest.
Arguments:
- features: bfloat16 [8192, 128], P(('row', 'rep')), may hold values from -6 to 6
- weight: bfloat16 [128, 256], P(None, 'feat'), may hold values from -0.5 to 0.5
- pair_tiles: int32 [16, 4, 8], P(('row', 'rep')), may hold values from 0 to 63, as said below
- pair_count: int32 [16, 4], P(('row', 'rep')), may hold values from 0 to 8, as said below
- tile_vals: bfloat16 [16, 4, 8, 128, 128], P(('row', 'rep')), may hold values from 0 to 1, as said below
- cotangent: bfloat16 [8192, 256], P(('row', 'rep'), 'feat'), may hold values from -0.0625 to 0.0625
Outputs:
- activated: bfloat16 [8192, 256], P(('row', 'rep'), 'feat')
- grad_weight: float32 [128, 256], P(None, 'feat')
The draws below stay inside these ranges and needn't reach their ends.
Inputs may be any that keep to these rules, and one draw needn't show every extreme that they name: The 8 positions of each list pair_tiles[b, j] are distinct. Every block b has an owner j with pair_count[b, j] = 8. `tile_vals`: entries are 0 or 1.
All inputs are finite; a program needn't handle non-finite values.
Results may differ from the reference program's by a relative error of at most 0.001.
Values may be sent and summed in bfloat16 or wider, within the bound.
No kernel may reach another device: no remote copies, remote signals or barrier semaphores. Data moves between devices by JAX's collectives and lax.ppermute only.
A program may use at most 128 MiB of HBM per device.

```python
import jax
import jax.numpy as jnp
from jax import lax

F_IN = 128
HID = 256
S = 512
TB = 128
MAXP = 8
BLOCKS = 16
NODES = 8192
N_ROW = 4
N_REP = 4


def draw_pair_count(key, part):
    key = jax.random.fold_in(key, 11)
    first_key, second_key, third_key = jax.random.split(key, 3)
    level = jax.random.randint(first_key, (BLOCKS, 1), 1, MAXP + 1)
    counts = jnp.minimum(jax.random.randint(second_key, (BLOCKS, N_ROW), 0, MAXP + 1), level)
    full_owner = jax.random.randint(third_key, (BLOCKS, 1), 0, N_ROW)
    owner_ids = jnp.arange(N_ROW)[None, :]
    return jnp.where(owner_ids == full_owner, MAXP, counts).astype(jnp.int32)


def draw_pair_tiles(key, part):
    key = jax.random.fold_in(key, 23)
    places = N_REP * (S // TB) * (S // TB)
    scores = jax.random.randint(key, (BLOCKS, N_ROW, places), 0, 1048576) * places
    scores = scores + jnp.arange(places)[None, None, :]
    order = jnp.argsort(scores, axis=-1)
    return order[:, :, :MAXP].astype(jnp.int32)


def draw_tile_vals(key, part):
    key = jax.random.fold_in(key, 37)
    picks = jax.random.randint(key, (BLOCKS, N_ROW, MAXP, TB, TB), 0, 64)
    ones = max(1, 256 // TB)
    return (picks < ones).astype(jnp.float32).astype(jnp.bfloat16)


def level_of(stream_key, extent, cuts, least, largest):
    def one(dim, shards_of):
        steps = jax.random.uniform(jax.random.fold_in(jax.random.fold_in(stream_key, 6), dim), (shards_of,), jnp.float32, least / len(cuts), largest / len(cuts))
        return jnp.repeat(jnp.exp(steps), extent[dim] // shards_of).reshape((-1,) + (1,) * (len(extent) - dim - 1))

    level = one(*cuts[0])
    for cut in cuts[1:]:
        level = level * one(*cut)
    return level


def scatter_about(key, dims, width, limit, cuts=(), held_as=jnp.bfloat16):
    result = jax.random.normal(key, dims, jnp.float32) * width
    if len(cuts) > 0:
        result = level_of(key, dims, cuts, -0.22, 0.18) * result
    return jnp.clip(result, min=-limit, max=limit).astype(held_as)


def setup_inputs(seed: int = 0) -> dict:
    streams_of = jax.random.split(jax.random.key(seed), 7)
    features = scatter_about(streams_of[0], (NODES, F_IN), 1.0, 6.0, ((0, 16),))
    weight = scatter_about(streams_of[1], (F_IN, HID), F_IN ** -0.5, 0.5, ((1, 2),))
    pair_tiles = draw_pair_tiles(jax.random.fold_in(streams_of[6], 71), 0)
    pair_count = draw_pair_count(jax.random.fold_in(streams_of[6], 71), 0)
    tile_vals = draw_tile_vals(jax.random.fold_in(streams_of[6], 71), 0)
    cotangent = scatter_about(streams_of[5], (NODES, HID), NODES ** -0.5, 0.0625, ((0, 16), (1, 2)))
    return dict(features=features, weight=weight, pair_tiles=pair_tiles, pair_count=pair_count, tile_vals=tile_vals, cotangent=cotangent)


highest = lax.Precision.HIGHEST

def aggregate(tile_vals, pair_tiles, pair_count, dataset):
    feat_width = dataset.shape[1]
    col_tiles = S // TB
    row_tiles = N_REP * col_tiles
    grouped = dataset.reshape(N_ROW, N_REP, col_tiles, TB, feat_width)
    owners = jnp.arange(N_ROW)
    slot_ids = jnp.arange(MAXP)
    tile_ids = jnp.arange(row_tiles)

    def one_block(block_row):
        summed = jnp.zeros((row_tiles, TB, feat_width), jnp.float32)
        degrees = jnp.zeros((row_tiles, TB), jnp.float32)
        for replica in range(N_REP):
            block_id = block_row * N_REP + replica
            positions = pair_tiles[block_id]
            active = (slot_ids[None, :] < pair_count[block_id][:, None]).astype(jnp.float32)
            entries = tile_vals[block_id].astype(jnp.float32) * active[:, :, None, None]
            sources = grouped[:, replica][owners[:, None], positions % col_tiles]
            products = jnp.einsum('jpuv,jpvf->jpuf', entries, sources, precision=highest)
            placing = (positions[:, :, None] // col_tiles == tile_ids).astype(jnp.float32)
            summed = summed + jnp.einsum('jpr,jpuf->ruf', placing, products, precision=highest)
            degrees = degrees + jnp.einsum('jpr,jpu->ru', placing, lax.optimization_barrier(jnp.sum(entries, axis=-1)), precision=highest)
        return (summed.reshape(row_tiles * TB, feat_width), degrees.reshape(row_tiles * TB))
    partials, degrees = lax.map(one_block, jnp.arange(N_ROW))
    return (partials.reshape(NODES, feat_width), degrees.reshape(NODES))

def reference(features, weight, pair_tiles, pair_count, tile_vals, cotangent):
    features_f32 = features.astype(jnp.float32)
    aggregated, degree_part = aggregate(tile_vals, pair_tiles, pair_count, features_f32)
    aggregated = aggregated + features_f32
    row_scale = lax.rsqrt(degree_part + 1.0)[:, None]
    preact = row_scale * jnp.dot(aggregated, weight.astype(jnp.float32), precision=highest)
    sigmoid_z = jax.nn.sigmoid(preact)
    activated = (preact * sigmoid_z).astype(jnp.bfloat16)
    slopes = row_scale * cotangent.astype(jnp.float32) * sigmoid_z * (1.0 + preact * (1.0 - sigmoid_z))
    grad_weight = jnp.dot(aggregated.T, slopes, precision=highest)
    return (activated, grad_weight)
```

```python
import functools

import jax
import jax.numpy as jnp
from jax import lax
from jax.experimental import pallas as pl
from jax.experimental.pallas import tpu as pltpu
from jax.sharding import PartitionSpec as P

f32 = jnp.float32
bf16 = jnp.bfloat16
LONGEST = 8


def vmem(n):
    return [pl.BlockSpec(memory_space=pltpu.VMEM)] * n


def smem(n):
    return [pl.BlockSpec(memory_space=pltpu.SMEM)] * n


def lower_half(shape):
    lane = lax.broadcasted_iota(jnp.int32, shape, len(shape) - 1)
    return lane < shape[-1] // 2


def pack_kernel(x_ref, out_ref):
    half = x_ref.shape[0] // 2
    width = x_ref.shape[1]
    first = lax.axis_index("feat") == 0
    top = x_ref[:half].astype(f32)
    low = x_ref[half:].astype(f32)
    kept = jnp.where(first, top, low)
    moved = pltpu.roll(jnp.where(first, low, top), width // 2, 1)
    left = lower_half(kept.shape)
    out_ref[...] = jnp.where(left == first, kept, moved).astype(bf16)


def spread(block_ref, at, sources_ref, tile):
    half = block_ref.shape[0] if at is None else block_ref.shape[1]
    x = (block_ref[...] if at is None else block_ref[at]).astype(f32)
    left = lower_half(x.shape)
    top = jnp.where(left, x, 0.0).astype(bf16)
    low = jnp.where(left, pltpu.roll(x, x.shape[1] // 2, 1), 0.0).astype(bf16)
    n = half // tile
    for c in range(n):
        sources_ref[c] = top[c * tile : (c + 1) * tile]
        sources_ref[n + c] = low[c * tile : (c + 1) * tile]


def add_tiles(j, tiles_ref, pos_ref, count_ref, sources_ref, acc_ref, col_tiles):
    spare = acc_ref.shape[0] - 1
    for p in range(tiles_ref.shape[1]):
        t = pos_ref[j, p]
        i = jnp.where(p < count_ref[0, j], t // col_tiles, spare)
        acc_ref[i] += jnp.dot(
            tiles_ref[j, p], sources_ref[t % col_tiles], preferred_element_type=f32
        )


def own_kernel(tiles_ref, pos_ref, count_ref, x_ref, acc_ref, deg_ref, sources_ref):
    n_own, slots, tile, _ = tiles_ref.shape
    col_tiles = sources_ref.shape[0]
    row_tiles = acc_ref.shape[0] - 1
    acc_ref[...] = jnp.zeros_like(acc_ref)
    spread(x_ref, None, sources_ref, tile)
    add_tiles(
        lax.axis_index("row"), tiles_ref, pos_ref, count_ref, sources_ref, acc_ref, col_tiles
    )
    lane = lax.broadcasted_iota(jnp.int32, (tile, 128), 1)

    def sums_of(j, total):
        for p in range(slots):
            i = jnp.where(p < count_ref[0, j], pos_ref[j, p] // col_tiles, -1)
            mark = (lane == i).astype(f32).astype(bf16)
            total = total + jnp.dot(tiles_ref[j, p], mark, preferred_element_type=f32)
        return total

    total = jnp.zeros((tile, 128), f32)
    if n_own <= LONGEST:
        for j in range(n_own):
            total = sums_of(j, total)
    else:
        total = lax.fori_loop(0, n_own, sums_of, total)
    deg_ref[...] = total.T[:row_tiles]


def fold_kernel(n_blocks, *refs):
    tiles_ref, pos_ref, count_ref, start_ref, deg_ref = refs[:5]
    blocks = refs[5 : 5 + n_blocks]
    outs = refs[5 + n_blocks : -2]
    acc_ref, sources_ref = refs[-2:]
    n_own, slots, tile, _ = tiles_ref.shape
    col_tiles = sources_ref.shape[0]
    me = lax.axis_index("row")
    rep = lax.axis_index("rep")
    acc_ref[...] = start_ref[...]
    if n_blocks == n_own - 1:
        for k, block in enumerate(blocks):
            j = lax.rem(me + n_own - 1 - k, n_own)
            spread(block, None, sources_ref, tile)
            add_tiles(j, tiles_ref, pos_ref, count_ref, sources_ref, acc_ref, col_tiles)
    else:

        @pl.loop(1, n_own)
        def _(k):
            j = lax.rem(me + k, n_own)
            spread(blocks[0], j, sources_ref, tile)
            add_tiles(j, tiles_ref, pos_ref, count_ref, sources_ref, acc_ref, col_tiles)

    n_rep = len(outs)
    for k, out in enumerate(outs):
        q = lax.rem(rep + k, n_rep)
        n = col_tiles // 2
        for c in range(n):
            top = acc_ref[q * col_tiles + c]
            low = acc_ref[q * col_tiles + n + c]
            out[c * tile : (c + 1) * tile] = jnp.where(
                lower_half(top.shape), top, pltpu.roll(low, top.shape[1] // 2, 1)
            )
        rows = out.shape[0] - n * tile
        out[n * tile :] = jnp.zeros((rows, out.shape[1]), f32)
        for c in range(col_tiles):
            out[n * tile + c : n * tile + c + 1] = deg_ref[pl.ds(q * col_tiles + c, 1)]


def sum_kernel(*refs):
    total = refs[0][...]
    for ref in refs[1:-1]:
        total = total + ref[...]
    refs[-1][...] = total


def split(x):
    high = x.astype(bf16)
    return high, (x - high.astype(f32)).astype(bf16)


def layer_kernel(mine_ref, other_ref, x_ref, w_ref, cot_ref, act_ref, grad_ref):
    half = other_ref.shape[0]
    width = other_ref.shape[1]
    tile = 128
    first = lax.axis_index("feat") == 0
    mine = mine_ref[:half]
    other = other_ref[...]
    here = jnp.where(first, mine, other)
    there = jnp.where(first, other, mine)
    left = lower_half(here.shape)
    top = jnp.where(left, here, pltpu.roll(there, width // 2, 1)) + x_ref[:half].astype(f32)
    low = jnp.where(left, pltpu.roll(here, width // 2, 1), there) + x_ref[half:].astype(f32)
    agg = jnp.concatenate([top, low], axis=0)
    scales = lax.rsqrt(mine_ref[half:] + 1.0)
    rows = scales.shape[0]
    turned = jnp.concatenate([scales] * (128 // rows), axis=0).T
    scale = jnp.concatenate(
        [jnp.broadcast_to(turned[:, c : c + 1], (tile, 128)) for c in range(2 * half // tile)],
        axis=0,
    )
    high, rest = split(agg)
    w = w_ref[...]
    preact = jnp.dot(high, w, preferred_element_type=f32)
    preact = scale * (preact + jnp.dot(rest, w, preferred_element_type=f32))
    sig = 1.0 / (1.0 + jnp.exp(-preact))
    act_ref[...] = (preact * sig).astype(bf16)
    slopes = scale * cot_ref[...].astype(f32) * sig * (1.0 + preact * (1.0 - sig))
    s_high, s_rest = split(slopes)

    def turned_dot(a, b):
        return lax.dot_general(a, b, (((0,), (0,)), ((), ())), preferred_element_type=f32)

    grad_ref[...] = (
        turned_dot(high, s_high) + turned_dot(high, s_rest) + turned_dot(rest, s_high)
    )


def shape(*dims, dtype=f32):
    return jax.ShapeDtypeStruct(dims, dtype)


def call(kernel, outs, in_specs, scratch=(), cost=None):
    return pl.pallas_call(
        kernel,
        out_shape=outs,
        in_specs=in_specs,
        out_specs=vmem(1)[0] if not isinstance(outs, (list, tuple)) else vmem(len(outs)),
        scratch_shapes=list(scratch),
        compiler_params=pltpu.CompilerParams(vmem_limit_bytes=48 * 1024 * 1024),
        cost_estimate=cost,
    )


def total_over(x, axis):
    n = lax.axis_size(axis)
    if n > LONGEST:
        return lax.psum(x, axis)
    parts = [lax.ppermute(x, axis, [(i, (i + k) % n) for i in range(n)]) for k in range(1, n)]
    return call(sum_kernel, shape(*x.shape), vmem(n))(x, *parts)


def shards(features, weight, pair_tiles, pair_count, tile_vals, cotangent):
    rows, width = features.shape
    _, n_own, slots, tile, _ = tile_vals.shape
    col_tiles = rows // tile
    half = rows // 2
    n_rep = lax.axis_size("rep")
    row_tiles = n_rep * col_tiles
    pos, counts, tiles = pair_tiles[0], pair_count, tile_vals[0]

    packed = call(pack_kernel, shape(half, width, dtype=bf16), vmem(1))(features)
    if n_own <= LONGEST:
        blocks = [
            lax.ppermute(packed, "row", [(i, (i + k) % n_own) for i in range(n_own)])
            for k in range(1, n_own)
        ]
    else:
        blocks = [lax.all_gather(packed, "row")]
    sources = pltpu.VMEM((col_tiles, tile, width), bf16)
    start, degrees = call(
        own_kernel,
        [shape(row_tiles + 1, tile, width), shape(row_tiles, tile)],
        vmem(1) + smem(2) + vmem(1),
        [sources],
        pl.CostEstimate(flops=10**8, bytes_accessed=3 * 10**6, transcendentals=0),
    )(tiles, pos, counts, packed)
    message = shape(half + 8, width)
    mine, *sends = call(
        functools.partial(fold_kernel, len(blocks)),
        [message] * n_rep,
        vmem(1) + smem(2) + vmem(2 + len(blocks)),
        [pltpu.VMEM((row_tiles + 1, tile, width), f32), sources],
    )(tiles, pos, counts, start, degrees, *blocks)
    parts = [
        lax.ppermute(sent, "rep", [(i, (i + k + 1) % n_rep) for i in range(n_rep)])
        for k, sent in enumerate(sends)
    ]
    mine = call(sum_kernel, message, vmem(n_rep))(mine, *parts)
    other = lax.ppermute(mine[:half], "feat", [(0, 1), (1, 0)])
    activated, grad = call(
        layer_kernel,
        [shape(rows, weight.shape[1], dtype=bf16), shape(width, weight.shape[1])],
        vmem(5),
    )(mine, other, features, weight, cotangent)
    grad = total_over(grad, "rep")
    grad = total_over(grad, "row")
    return activated, grad


def solution(mesh):
    return jax.shard_map(
        shards,
        mesh=mesh,
        in_specs=(
            P(("row", "rep"), None),
            P(None, "feat"),
            P(("row", "rep"), None, None),
            P(("row", "rep"), None),
            P(("row", "rep"), None, None, None, None),
            P(("row", "rep"), "feat"),
        ),
        out_specs=(P(("row", "rep"), "feat"), P(None, "feat")),
        check_vma=False,
    )
```

```python
import functools

import jax
import jax.numpy as jnp
from jax import lax
from jax.experimental import pallas as pl
from jax.experimental.pallas import tpu as pltpu
from jax.sharding import PartitionSpec as P

f32 = jnp.float32
bf16 = jnp.bfloat16
LONGEST = 8
ORDER = (0, 3, 2, 1)


def vmem(n):
    return [pl.BlockSpec(memory_space=pltpu.VMEM)] * n


def lower_half(shape):
    lane = lax.broadcasted_iota(jnp.int32, shape, len(shape) - 1)
    return lane < shape[-1] // 2


def pack_kernel(x_ref, out_ref):
    half = x_ref.shape[0] // 2
    width = x_ref.shape[1]
    first = lax.axis_index("feat") == 0
    top = x_ref[:half].astype(f32)
    low = x_ref[half:].astype(f32)
    kept = jnp.where(first, top, low)
    moved = pltpu.roll(jnp.where(first, low, top), width // 2, 1)
    left = lower_half(kept.shape)
    out_ref[...] = jnp.where(left == first, kept, moved).astype(bf16)


def spread(x, sources_ref, tile):
    x = x.astype(f32)
    left = lower_half(x.shape)
    top = jnp.where(left, x, 0.0).astype(bf16)
    low = jnp.where(left, pltpu.roll(x, x.shape[1] // 2, 1), 0.0).astype(bf16)
    n = x.shape[0] // tile
    for c in range(n):
        sources_ref[c] = top[c * tile : (c + 1) * tile]
        sources_ref[n + c] = low[c * tile : (c + 1) * tile]


def add_tiles(j, tiles_ref, pos_ref, count_ref, sources_ref, acc_ref):
    col_tiles = sources_ref.shape[0]
    spare = acc_ref.shape[0] - 1
    listed = pos_ref[pl.ds(j, 1)]
    live = jnp.sum(
        jnp.where(lax.broadcasted_iota(jnp.int32, count_ref.shape, 1) == j, count_ref[...], 0)
    )
    for p in range(tiles_ref.shape[1]):
        t = listed[0, p]
        i = jnp.where(p < live, t // col_tiles, spare)
        acc_ref[i] += jnp.dot(
            tiles_ref[j, p], sources_ref[t % col_tiles], preferred_element_type=f32
        )


def own_kernel(tiles_ref, pos_ref, count_ref, x_ref, acc_ref, deg_ref, sources_ref):
    n_own, slots, tile, _ = tiles_ref.shape
    col_tiles = sources_ref.shape[0]
    row_tiles = acc_ref.shape[0] - 1
    acc_ref[...] = jnp.zeros_like(acc_ref)
    spread(x_ref[...], sources_ref, tile)
    add_tiles(lax.axis_index("row"), tiles_ref, pos_ref, count_ref, sources_ref, acc_ref)
    lane = lax.broadcasted_iota(jnp.int32, (tile, 128), 1)

    slot = lax.broadcasted_iota(jnp.int32, (1, slots), 1)
    owner = lax.broadcasted_iota(jnp.int32, count_ref.shape, 1)

    def sums_of(j, total):
        live = jnp.sum(jnp.where(owner == j, count_ref[...], 0), axis=1, keepdims=True)
        rows = jnp.where(slot < live, pos_ref[pl.ds(j, 1)] // col_tiles, -1)
        for p in range(slots):
            mark = (lane == rows[:, p : p + 1]).astype(f32).astype(bf16)
            total = total + jnp.dot(tiles_ref[j, p], mark, preferred_element_type=f32)
        return total

    total = jnp.zeros((tile, 128), f32)
    if n_own <= LONGEST:
        for j in range(n_own):
            total = sums_of(j, total)
    else:
        total = lax.fori_loop(0, n_own, sums_of, total)
    deg_ref[...] = total.T[:row_tiles]


def fold_kernel(step, tiles_ref, pos_ref, count_ref, block_ref, start_ref, acc_ref, sources_ref):
    tile = tiles_ref.shape[2]
    spread(block_ref[...], sources_ref, tile)
    j = sender(step, lax.axis_index("row"))
    add_tiles(j, tiles_ref, pos_ref, count_ref, sources_ref, acc_ref)


def fold_all_kernel(tiles_ref, pos_ref, count_ref, blocks_ref, start_ref, acc_ref, sources_ref):
    n_own, _, tile, _ = tiles_ref.shape
    me = lax.axis_index("row")

    @pl.loop(1, n_own)
    def _(k):
        j = lax.rem(me + k, n_own)
        spread(blocks_ref[j], sources_ref, tile)
        add_tiles(j, tiles_ref, pos_ref, count_ref, sources_ref, acc_ref)


def send_kernel(acc_ref, deg_ref, *outs):
    tile, width = acc_ref.shape[1:]
    row_tiles = acc_ref.shape[0] - 1
    rep = lax.axis_index("rep")
    n_rep = len(outs)
    col_tiles = row_tiles // n_rep
    n = col_tiles // 2
    left = lower_half((tile, width))
    for k, out in enumerate(outs):
        q = rep ^ ORDER[k] if n_rep == 4 else lax.rem(rep + k, n_rep)
        for c in range(n):
            top = acc_ref[q * col_tiles + c]
            low = acc_ref[q * col_tiles + n + c]
            out[c * tile : (c + 1) * tile] = jnp.where(left, top, pltpu.roll(low, width // 2, 1))
        rows = out.shape[0] - n * tile
        out[n * tile :] = jnp.zeros((rows, width), f32)
        for c in range(col_tiles):
            out[n * tile + c : n * tile + c + 1] = deg_ref[pl.ds(q * col_tiles + c, 1)]


def last_kernel(step, *refs):
    acc_ref, sources_ref = refs[-2:]
    tiles_ref, pos_ref, count_ref, block_ref, start_ref, deg_ref = refs[:6]
    acc_ref[...] = start_ref[...]
    spread(block_ref[...], sources_ref, tiles_ref.shape[2])
    j = sender(step, lax.axis_index("row"))
    add_tiles(j, tiles_ref, pos_ref, count_ref, sources_ref, acc_ref)
    send_kernel(acc_ref, deg_ref, *refs[6:-2])


def copy_kernel(x_ref, out_ref):
    out_ref[...] = x_ref[...]


def sum_kernel(*refs):
    total = refs[0][...]
    for ref in refs[1:-1]:
        total = total + ref[...]
    refs[-1][...] = total


def split(x):
    high = x.astype(bf16)
    return high, (x - high.astype(f32)).astype(bf16)


def layer_kernel(mine_ref, other_ref, x_ref, w_ref, cot_ref, act_ref, grad_ref):
    half = other_ref.shape[0]
    width = other_ref.shape[1]
    tile = 128
    first = lax.axis_index("feat") == 0
    mine = mine_ref[:half]
    other = other_ref[...]
    here = jnp.where(first, mine, other)
    there = jnp.where(first, other, mine)
    left = lower_half(here.shape)
    top = jnp.where(left, here, pltpu.roll(there, width // 2, 1)) + x_ref[:half].astype(f32)
    low = jnp.where(left, pltpu.roll(here, width // 2, 1), there) + x_ref[half:].astype(f32)
    agg = jnp.concatenate([top, low], axis=0)
    scales = lax.rsqrt(mine_ref[half:] + 1.0)
    rows = scales.shape[0]
    turned = jnp.concatenate([scales] * (128 // rows), axis=0).T
    scale = jnp.concatenate(
        [jnp.broadcast_to(turned[:, c : c + 1], (tile, 128)) for c in range(2 * half // tile)],
        axis=0,
    )
    high, rest = split(agg)
    w = w_ref[...]
    preact = jnp.dot(high, w, preferred_element_type=f32)
    preact = scale * (preact + jnp.dot(rest, w, preferred_element_type=f32))
    sig = 1.0 / (1.0 + jnp.exp(-preact))
    act_ref[...] = (preact * sig).astype(bf16)
    slopes = scale * cot_ref[...].astype(f32) * sig * (1.0 + preact * (1.0 - sig))
    s_high, s_rest = split(slopes)

    def turned_dot(a, b):
        return lax.dot_general(a, b, (((0,), (0,)), ((), ())), preferred_element_type=f32)

    grad_ref[...] = (
        turned_dot(high, s_high) + turned_dot(high, s_rest) + turned_dot(rest, s_high)
    )


def shape(*dims, dtype=f32):
    return jax.ShapeDtypeStruct(dims, dtype)


def call(kernel, outs, in_specs, scratch=(), cost=None, aliases=None):
    return pl.pallas_call(
        kernel,
        out_shape=outs,
        in_specs=in_specs,
        out_specs=vmem(1)[0] if not isinstance(outs, (list, tuple)) else vmem(len(outs)),
        scratch_shapes=list(scratch),
        compiler_params=pltpu.CompilerParams(vmem_limit_bytes=48 * 1024 * 1024),
        cost_estimate=cost,
        input_output_aliases=aliases or {},
    )


def pairs(n, k):
    return [(i, i ^ k) for i in range(n)]


def steps(n):
    if n == 4:
        return [(2, 3, 1, 0), (3, 2, 0, 1), (1, 0, 3, 2)]
    return [tuple(i ^ k for i in range(n)) for k in range(n - 1, 0, -1)]


def sender(step, me):
    j = jnp.int32(0)
    for i, target in enumerate(step):
        j = jnp.where(me == target, i, j)
    return j


def total_over(x, axis):
    n = lax.axis_size(axis)
    if n > LONGEST:
        return lax.psum(x, axis)
    parts = [lax.ppermute(x, axis, pairs(n, k)) for k in range(n - 1, 0, -1)]
    return call(sum_kernel, shape(*x.shape), vmem(n))(x, *parts)


def shards(features, weight, pair_tiles, pair_count, tile_vals, cotangent):
    rows, width = features.shape
    _, n_own, slots, tile, _ = tile_vals.shape
    col_tiles = rows // tile
    half = rows // 2
    n_rep = lax.axis_size("rep")
    row_tiles = n_rep * col_tiles
    pos, counts, tiles = pair_tiles[0], pair_count, tile_vals[0]

    packed = call(
        pack_kernel,
        shape(half, width, dtype=bf16),
        vmem(1),
        cost=pl.CostEstimate(flops=0, bytes_accessed=10**7, transcendentals=0),
    )(features)
    if n_own <= LONGEST:
        blocks = [
            lax.ppermute(packed, "row", list(enumerate(step))) for step in steps(n_own)
        ]
    else:
        blocks = [lax.all_gather(packed, "row")]
    sources = pltpu.VMEM((col_tiles, tile, width), bf16)
    lists = vmem(3)
    cost = pl.CostEstimate(flops=10**8, bytes_accessed=3 * 10**6, transcendentals=0)
    total_shape = shape(row_tiles + 1, tile, width)
    total, degrees = call(
        own_kernel,
        [total_shape, shape(row_tiles, tile)],
        lists + vmem(1),
        [sources],
        cost,
    )(tiles, pos, counts, packed)
    messages = [shape(half + 8, width)] * n_rep
    if n_own <= LONGEST:
        for step, block in zip(steps(n_own)[:-1], blocks):
            total = call(
                functools.partial(fold_kernel, step),
                total_shape,
                lists + vmem(2),
                [sources],
                cost,
                {4: 0},
            )(tiles, pos, counts, block, total)
        mine, *sends = call(
            functools.partial(last_kernel, steps(n_own)[-1]),
            messages,
            lists + vmem(3),
            [pltpu.VMEM(total_shape.shape, f32), sources],
        )(tiles, pos, counts, blocks[-1], total, degrees)
    else:
        total = call(fold_all_kernel, total_shape, lists + vmem(2), [sources], cost, {4: 0})(
            tiles, pos, counts, blocks[0], total
        )
        mine, *sends = call(send_kernel, messages, vmem(2))(total, degrees)
    parts = [
        lax.ppermute(sent, "rep", pairs(n_rep, ORDER[k + 1]))
        for k, sent in enumerate(sends)
    ]
    mine = call(sum_kernel, messages[0], vmem(n_rep))(mine, *parts)
    other = lax.ppermute(mine[:half], "feat", [(0, 1), (1, 0)])
    activated_shape = shape(rows, weight.shape[1], dtype=bf16)
    activated, grad = call(
        layer_kernel,
        [activated_shape, shape(width, weight.shape[1])],
        vmem(5),
    )(mine, other, features, weight, cotangent)
    grad = total_over(grad, "rep")
    grad = total_over(grad, "row")
    activated = call(copy_kernel, activated_shape, vmem(1))(activated)
    return activated, grad


def solution(mesh):
    return jax.shard_map(
        shards,
        mesh=mesh,
        in_specs=(
            P(("row", "rep"), None),
            P(None, "feat"),
            P(("row", "rep"), None, None),
            P(("row", "rep"), None),
            P(("row", "rep"), None, None, None, None),
            P(("row", "rep"), "feat"),
        ),
        out_specs=(P(("row", "rep"), "feat"), P(None, "feat")),
        check_vma=False,
    )
```

```python
import functools

import jax
import jax.numpy as jnp
from jax import lax
from jax.experimental import pallas as pl
from jax.experimental.pallas import tpu as pltpu
from jax.sharding import PartitionSpec as P

f32 = jnp.float32
bf16 = jnp.bfloat16
LONGEST = 8
STEPS = [(2, 3, 1, 0), (1, 0, 3, 2), (3, 2, 0, 1)]


def vmem(n):
    return [pl.BlockSpec(memory_space=pltpu.VMEM)] * n


def lower_half(shape):
    lane = lax.broadcasted_iota(jnp.int32, shape, len(shape) - 1)
    return lane < shape[-1] // 2


def pack_kernel(x_ref, out_ref):
    half = x_ref.shape[0] // 2
    width = x_ref.shape[1]
    first = lax.axis_index("feat") == 0
    top = x_ref[:half].astype(f32)
    low = x_ref[half:].astype(f32)
    kept = jnp.where(first, top, low)
    moved = pltpu.roll(jnp.where(first, low, top), width // 2, 1)
    left = lower_half(kept.shape)
    out_ref[...] = jnp.where(left == first, kept, moved).astype(bf16)


def spread(x, sources_ref, tile):
    x = x.astype(f32)
    left = lower_half(x.shape)
    top = jnp.where(left, x, 0.0).astype(bf16)
    low = jnp.where(left, pltpu.roll(x, x.shape[1] // 2, 1), 0.0).astype(bf16)
    n = x.shape[0] // tile
    for c in range(n):
        sources_ref[c] = top[c * tile : (c + 1) * tile]
        sources_ref[n + c] = low[c * tile : (c + 1) * tile]


def add_tiles(j, tiles_ref, pos_ref, count_ref, sources_ref, acc_ref):
    col_tiles = sources_ref.shape[0]
    spare = acc_ref.shape[0] - 1
    listed = pos_ref[pl.ds(j, 1)]
    live = jnp.sum(
        jnp.where(lax.broadcasted_iota(jnp.int32, count_ref.shape, 1) == j, count_ref[...], 0)
    )
    for p in range(tiles_ref.shape[1]):
        t = listed[0, p]
        i = jnp.where(p < live, t // col_tiles, spare)
        acc_ref[i] += jnp.dot(
            tiles_ref[j, p], sources_ref[t % col_tiles], preferred_element_type=f32
        )


def own_kernel(tiles_ref, pos_ref, count_ref, x_ref, acc_ref, deg_ref, sources_ref):
    n_own, slots, tile, _ = tiles_ref.shape
    col_tiles = sources_ref.shape[0]
    row_tiles = acc_ref.shape[0] - 1
    acc_ref[...] = jnp.zeros_like(acc_ref)
    spread(x_ref[...], sources_ref, tile)
    add_tiles(lax.axis_index("row"), tiles_ref, pos_ref, count_ref, sources_ref, acc_ref)
    lane = lax.broadcasted_iota(jnp.int32, (tile, 128), 1)

    slot = lax.broadcasted_iota(jnp.int32, (1, slots), 1)
    owner = lax.broadcasted_iota(jnp.int32, count_ref.shape, 1)

    def sums_of(j, total):
        live = jnp.sum(jnp.where(owner == j, count_ref[...], 0), axis=1, keepdims=True)
        rows = jnp.where(slot < live, pos_ref[pl.ds(j, 1)] // col_tiles, -1)
        for p in range(slots):
            mark = (lane == rows[:, p : p + 1]).astype(f32).astype(bf16)
            total = total + jnp.dot(tiles_ref[j, p], mark, preferred_element_type=f32)
        return total

    total = jnp.zeros((tile, 128), f32)
    if n_own <= LONGEST:
        for j in range(n_own):
            total = sums_of(j, total)
    else:
        total = lax.fori_loop(0, n_own, sums_of, total)
    deg_ref[...] = total.T[:row_tiles]


def fold_kernel(step, tiles_ref, pos_ref, count_ref, block_ref, start_ref, acc_ref, sources_ref):
    tile = tiles_ref.shape[2]
    spread(block_ref[...], sources_ref, tile)
    j = sender(step, lax.axis_index("row"))
    add_tiles(j, tiles_ref, pos_ref, count_ref, sources_ref, acc_ref)


def fold_all_kernel(tiles_ref, pos_ref, count_ref, blocks_ref, start_ref, acc_ref, sources_ref):
    n_own, _, tile, _ = tiles_ref.shape
    me = lax.axis_index("row")

    @pl.loop(1, n_own)
    def _(k):
        j = lax.rem(me + k, n_own)
        spread(blocks_ref[j], sources_ref, tile)
        add_tiles(j, tiles_ref, pos_ref, count_ref, sources_ref, acc_ref)


def send_kernel(acc_ref, deg_ref, *outs):
    tile, width = acc_ref.shape[1:]
    row_tiles = acc_ref.shape[0] - 1
    rep = lax.axis_index("rep")
    n_rep = len(outs)
    col_tiles = row_tiles // n_rep
    n = col_tiles // 2
    left = lower_half((tile, width))
    for k, out in enumerate(outs):
        q = rep if k == 0 else target(steps(n_rep)[k - 1], rep)
        for c in range(n):
            top = acc_ref[q * col_tiles + c]
            low = acc_ref[q * col_tiles + n + c]
            out[c * tile : (c + 1) * tile] = jnp.where(left, top, pltpu.roll(low, width // 2, 1))
        rows = out.shape[0] - n * tile
        out[n * tile :] = jnp.zeros((rows, width), f32)
        for c in range(col_tiles):
            out[n * tile + c : n * tile + c + 1] = deg_ref[pl.ds(q * col_tiles + c, 1)]


def last_kernel(step, *refs):
    acc_ref, sources_ref = refs[-2:]
    tiles_ref, pos_ref, count_ref, block_ref, start_ref, deg_ref = refs[:6]
    acc_ref[...] = start_ref[...]
    spread(block_ref[...], sources_ref, tiles_ref.shape[2])
    j = sender(step, lax.axis_index("row"))
    add_tiles(j, tiles_ref, pos_ref, count_ref, sources_ref, acc_ref)
    send_kernel(acc_ref, deg_ref, *refs[6:-2])


def copy_kernel(x_ref, out_ref):
    out_ref[...] = x_ref[...]


def sum_kernel(*refs):
    total = refs[0][...]
    for ref in refs[1:-1]:
        total = total + ref[...]
    refs[-1][...] = total


def split(x):
    high = x.astype(bf16)
    return high, (x - high.astype(f32)).astype(bf16)


def layer_kernel(mine_ref, other_ref, x_ref, w_ref, cot_ref, act_ref, grad_ref):
    half = other_ref.shape[0]
    width = other_ref.shape[1]
    tile = 128
    first = lax.axis_index("feat") == 0
    mine = mine_ref[:half]
    other = other_ref[...]
    here = jnp.where(first, mine, other)
    there = jnp.where(first, other, mine)
    left = lower_half(here.shape)
    top = jnp.where(left, here, pltpu.roll(there, width // 2, 1)) + x_ref[:half].astype(f32)
    low = jnp.where(left, pltpu.roll(here, width // 2, 1), there) + x_ref[half:].astype(f32)
    agg = jnp.concatenate([top, low], axis=0)
    scales = lax.rsqrt(mine_ref[half:] + 1.0)
    rows = scales.shape[0]
    turned = jnp.concatenate([scales] * (128 // rows), axis=0).T
    scale = jnp.concatenate(
        [jnp.broadcast_to(turned[:, c : c + 1], (tile, 128)) for c in range(2 * half // tile)],
        axis=0,
    )
    high, rest = split(agg)
    w = w_ref[...]
    preact = jnp.dot(high, w, preferred_element_type=f32)
    preact = scale * (preact + jnp.dot(rest, w, preferred_element_type=f32))
    sig = 1.0 / (1.0 + jnp.exp(-preact))
    act_ref[...] = (preact * sig).astype(bf16)
    slopes = scale * cot_ref[...].astype(f32) * sig * (1.0 + preact * (1.0 - sig))
    s_high, s_rest = split(slopes)

    def turned_dot(a, b):
        return lax.dot_general(a, b, (((0,), (0,)), ((), ())), preferred_element_type=f32)

    grad_ref[...] = (
        turned_dot(high, s_high) + turned_dot(high, s_rest) + turned_dot(rest, s_high)
    )


def shape(*dims, dtype=f32):
    return jax.ShapeDtypeStruct(dims, dtype)


def call(kernel, outs, in_specs, scratch=(), cost=None, aliases=None):
    return pl.pallas_call(
        kernel,
        out_shape=outs,
        in_specs=in_specs,
        out_specs=vmem(1)[0] if not isinstance(outs, (list, tuple)) else vmem(len(outs)),
        scratch_shapes=list(scratch),
        compiler_params=pltpu.CompilerParams(vmem_limit_bytes=48 * 1024 * 1024),
        cost_estimate=cost,
        input_output_aliases=aliases or {},
    )


def steps(n):
    if n == 4:
        return STEPS
    return [tuple(i ^ k for i in range(n)) for k in range(n - 1, 0, -1)]


def target(step, me):
    j = jnp.int32(0)
    for i, to in enumerate(step):
        j = jnp.where(me == i, to, j)
    return j


def sender(step, me):
    j = jnp.int32(0)
    for i, target in enumerate(step):
        j = jnp.where(me == target, i, j)
    return j


def total_over(x, axis):
    n = lax.axis_size(axis)
    if n > LONGEST:
        return lax.psum(x, axis)
    parts = [lax.ppermute(x, axis, list(enumerate(step))) for step in steps(n)]
    return call(sum_kernel, shape(*x.shape), vmem(n))(x, *parts)


def shards(features, weight, pair_tiles, pair_count, tile_vals, cotangent):
    rows, width = features.shape
    _, n_own, slots, tile, _ = tile_vals.shape
    col_tiles = rows // tile
    half = rows // 2
    n_rep = lax.axis_size("rep")
    row_tiles = n_rep * col_tiles
    pos, counts, tiles = pair_tiles[0], pair_count, tile_vals[0]

    packed = call(
        pack_kernel,
        shape(half, width, dtype=bf16),
        vmem(1),
        cost=pl.CostEstimate(flops=0, bytes_accessed=10**7, transcendentals=0),
    )(features)
    if n_own <= LONGEST:
        blocks = [
            lax.ppermute(packed, "row", list(enumerate(step))) for step in steps(n_own)
        ]
    else:
        blocks = [lax.all_gather(packed, "row")]
    sources = pltpu.VMEM((col_tiles, tile, width), bf16)
    lists = vmem(3)
    cost = pl.CostEstimate(flops=10**8, bytes_accessed=3 * 10**6, transcendentals=0)
    total_shape = shape(row_tiles + 1, tile, width)
    total, degrees = call(
        own_kernel,
        [total_shape, shape(row_tiles, tile)],
        lists + vmem(1),
        [sources],
        cost,
    )(tiles, pos, counts, packed)
    messages = [shape(half + 8, width)] * n_rep
    if n_own <= LONGEST:
        for step, block in zip(steps(n_own)[:-1], blocks):
            total = call(
                functools.partial(fold_kernel, step),
                total_shape,
                lists + vmem(2),
                [sources],
                cost,
                {4: 0},
            )(tiles, pos, counts, block, total)
        mine, *sends = call(
            functools.partial(last_kernel, steps(n_own)[-1]),
            messages,
            lists + vmem(3),
            [pltpu.VMEM(total_shape.shape, f32), sources],
        )(tiles, pos, counts, blocks[-1], total, degrees)
    else:
        total = call(fold_all_kernel, total_shape, lists + vmem(2), [sources], cost, {4: 0})(
            tiles, pos, counts, blocks[0], total
        )
        mine, *sends = call(send_kernel, messages, vmem(2))(total, degrees)
    parts = [
        lax.ppermute(sent, "rep", list(enumerate(step)))
        for step, sent in zip(steps(n_rep), sends)
    ]
    mine = call(sum_kernel, messages[0], vmem(n_rep))(mine, *parts)
    other = lax.ppermute(mine[:half], "feat", [(0, 1), (1, 0)])
    activated_shape = shape(rows, weight.shape[1], dtype=bf16)
    activated, grad = call(
        layer_kernel,
        [activated_shape, shape(width, weight.shape[1])],
        vmem(5),
    )(mine, other, features, weight, cotangent)
    grad = total_over(grad, "rep")
    grad = total_over(grad, "row")
    activated = call(copy_kernel, activated_shape, vmem(1))(activated)
    return activated, grad


def solution(mesh):
    return jax.shard_map(
        shards,
        mesh=mesh,
        in_specs=(
            P(("row", "rep"), None),
            P(None, "feat"),
            P(("row", "rep"), None, None),
            P(("row", "rep"), None),
            P(("row", "rep"), None, None, None, None),
            P(("row", "rep"), "feat"),
        ),
        out_specs=(P(("row", "rep"), "feat"), P(None, "feat")),
        check_vma=False,
    )
```

```python
import functools

import jax
import jax.numpy as jnp
from jax import lax
from jax.experimental import pallas as pl
from jax.experimental.pallas import tpu as pltpu
from jax.sharding import PartitionSpec as P

f32 = jnp.float32
bf16 = jnp.bfloat16
LONGEST = 8
STEPS = {
    "gather": [(2, 3, 1, 0), (1, 0, 3, 2), (3, 2, 0, 1)],
    "partials": [(3, 2, 1, 0), (1, 3, 0, 2), (2, 0, 3, 1)],
    "rep": [(2, 3, 1, 0), (1, 0, 3, 2), (3, 2, 0, 1)],
    "row": [(2, 3, 1, 0), (1, 0, 3, 2), (3, 2, 0, 1)],
}


def vmem(n):
    return [pl.BlockSpec(memory_space=pltpu.VMEM)] * n


def lower_half(shape):
    lane = lax.broadcasted_iota(jnp.int32, shape, len(shape) - 1)
    return lane < shape[-1] // 2


def pack_kernel(x_ref, out_ref):
    half = x_ref.shape[0] // 2
    width = x_ref.shape[1]
    first = lax.axis_index("feat") == 0
    top = x_ref[:half].astype(f32)
    low = x_ref[half:].astype(f32)
    kept = jnp.where(first, top, low)
    moved = pltpu.roll(jnp.where(first, low, top), width // 2, 1)
    left = lower_half(kept.shape)
    out_ref[...] = jnp.where(left == first, kept, moved).astype(bf16)


def spread(x, sources_ref, tile):
    x = x.astype(f32)
    left = lower_half(x.shape)
    top = jnp.where(left, x, 0.0).astype(bf16)
    low = jnp.where(left, pltpu.roll(x, x.shape[1] // 2, 1), 0.0).astype(bf16)
    n = x.shape[0] // tile
    for c in range(n):
        sources_ref[c] = top[c * tile : (c + 1) * tile]
        sources_ref[n + c] = low[c * tile : (c + 1) * tile]


def add_tiles(j, tiles_ref, list_ref, sources_ref, acc_ref):
    col_tiles = sources_ref.shape[0]
    spare = acc_ref.shape[0] - 1
    listed = list_ref[pl.ds(j, 1)]
    for p in range(tiles_ref.shape[1]):
        t = listed[0, p]
        i = jnp.where(t < 0, spare, t // col_tiles)
        acc_ref[i] += jnp.dot(
            tiles_ref[j, p], sources_ref[jnp.maximum(t, 0) % col_tiles], preferred_element_type=f32
        )


def own_kernel(tiles_ref, list_ref, x_ref, acc_ref, deg_ref, sources_ref):
    n_own, slots, tile, _ = tiles_ref.shape
    col_tiles = sources_ref.shape[0]
    row_tiles = acc_ref.shape[0] - 1
    acc_ref[...] = jnp.zeros_like(acc_ref)
    spread(x_ref[...], sources_ref, tile)
    add_tiles(lax.axis_index("row"), tiles_ref, list_ref, sources_ref, acc_ref)
    lane = lax.broadcasted_iota(jnp.int32, (tile, 128), 1)


    def sums_of(j, total):
        listed = list_ref[pl.ds(j, 1)]
        rows = jnp.where(listed < 0, -1, listed // col_tiles)
        for p in range(slots):
            mark = (lane == rows[:, p : p + 1]).astype(f32).astype(bf16)
            total = total + jnp.dot(tiles_ref[j, p], mark, preferred_element_type=f32)
        return total

    total = jnp.zeros((tile, 128), f32)
    if n_own <= LONGEST:
        for j in range(n_own):
            total = sums_of(j, total)
    else:
        total = lax.fori_loop(0, n_own, sums_of, total)
    deg_ref[...] = total.T[:row_tiles]


def fold_kernel(step, tiles_ref, list_ref, block_ref, start_ref, acc_ref, sources_ref):
    tile = tiles_ref.shape[2]
    spread(block_ref[...], sources_ref, tile)
    j = sender(step, lax.axis_index("row"))
    add_tiles(j, tiles_ref, list_ref, sources_ref, acc_ref)


def fold_all_kernel(tiles_ref, list_ref, blocks_ref, start_ref, acc_ref, sources_ref):
    n_own, _, tile, _ = tiles_ref.shape
    me = lax.axis_index("row")

    @pl.loop(1, n_own)
    def _(k):
        j = lax.rem(me + k, n_own)
        spread(blocks_ref[j], sources_ref, tile)
        add_tiles(j, tiles_ref, list_ref, sources_ref, acc_ref)


def send_kernel(acc_ref, deg_ref, *outs):
    tile, width = acc_ref.shape[1:]
    row_tiles = acc_ref.shape[0] - 1
    rep = lax.axis_index("rep")
    n_rep = len(outs)
    col_tiles = row_tiles // n_rep
    n = col_tiles // 2
    left = lower_half((tile, width))
    for k, out in enumerate(outs):
        q = rep if k == 0 else target(steps(n_rep, "partials")[k - 1], rep)
        for c in range(n):
            top = acc_ref[q * col_tiles + c]
            low = acc_ref[q * col_tiles + n + c]
            out[c * tile : (c + 1) * tile] = jnp.where(left, top, pltpu.roll(low, width // 2, 1))
        rows = out.shape[0] - n * tile
        out[n * tile :] = jnp.zeros((rows, width), f32)
        for c in range(col_tiles):
            out[n * tile + c : n * tile + c + 1] = deg_ref[pl.ds(q * col_tiles + c, 1)]


def last_kernel(step, *refs):
    acc_ref, sources_ref = refs[-2:]
    tiles_ref, list_ref, block_ref, start_ref, deg_ref = refs[:5]
    acc_ref[...] = start_ref[...]
    spread(block_ref[...], sources_ref, tiles_ref.shape[2])
    j = sender(step, lax.axis_index("row"))
    add_tiles(j, tiles_ref, list_ref, sources_ref, acc_ref)
    send_kernel(acc_ref, deg_ref, *refs[5:-2])


def copy_kernel(x_ref, out_ref):
    out_ref[...] = x_ref[...]


def sum_kernel(*refs):
    total = refs[0][...]
    for ref in refs[1:-1]:
        total = total + ref[...]
    refs[-1][...] = total


def split(x):
    high = x.astype(bf16)
    return high, (x - high.astype(f32)).astype(bf16)


def layer_kernel(mine_ref, other_ref, x_ref, w_ref, cot_ref, act_ref, grad_ref):
    half = other_ref.shape[0]
    width = other_ref.shape[1]
    tile = 128
    first = lax.axis_index("feat") == 0
    mine = mine_ref[:half]
    other = other_ref[...]
    here = jnp.where(first, mine, other)
    there = jnp.where(first, other, mine)
    left = lower_half(here.shape)
    top = jnp.where(left, here, pltpu.roll(there, width // 2, 1)) + x_ref[:half].astype(f32)
    low = jnp.where(left, pltpu.roll(here, width // 2, 1), there) + x_ref[half:].astype(f32)
    agg = jnp.concatenate([top, low], axis=0)
    scales = lax.rsqrt(mine_ref[half:] + 1.0)
    rows = scales.shape[0]
    turned = jnp.concatenate([scales] * (128 // rows), axis=0).T
    scale = jnp.concatenate(
        [jnp.broadcast_to(turned[:, c : c + 1], (tile, 128)) for c in range(2 * half // tile)],
        axis=0,
    )
    high, rest = split(agg)
    w = w_ref[...]
    preact = jnp.dot(high, w, preferred_element_type=f32)
    preact = scale * (preact + jnp.dot(rest, w, preferred_element_type=f32))
    sig = 1.0 / (1.0 + jnp.exp(-preact))
    act_ref[...] = (preact * sig).astype(bf16)
    slopes = scale * cot_ref[...].astype(f32) * sig * (1.0 + preact * (1.0 - sig))
    s_high, s_rest = split(slopes)

    def turned_dot(a, b):
        return lax.dot_general(a, b, (((0,), (0,)), ((), ())), preferred_element_type=f32)

    grad_ref[...] = (
        turned_dot(high, s_high) + turned_dot(high, s_rest) + turned_dot(rest, s_high)
    )


def shape(*dims, dtype=f32):
    return jax.ShapeDtypeStruct(dims, dtype)


def call(kernel, outs, in_specs, scratch=(), cost=None, aliases=None):
    return pl.pallas_call(
        kernel,
        out_shape=outs,
        in_specs=in_specs,
        out_specs=vmem(1)[0] if not isinstance(outs, (list, tuple)) else vmem(len(outs)),
        scratch_shapes=list(scratch),
        compiler_params=pltpu.CompilerParams(vmem_limit_bytes=48 * 1024 * 1024),
        cost_estimate=cost,
        input_output_aliases=aliases or {},
    )


def steps(n, phase):
    if n == 4:
        return STEPS[phase]
    return [tuple(i ^ k for i in range(n)) for k in range(n - 1, 0, -1)]


def target(step, me):
    j = jnp.int32(0)
    for i, to in enumerate(step):
        j = jnp.where(me == i, to, j)
    return j


def sender(step, me):
    j = jnp.int32(0)
    for i, target in enumerate(step):
        j = jnp.where(me == target, i, j)
    return j


def total_over(x, axis):
    n = lax.axis_size(axis)
    if n > LONGEST:
        return lax.psum(x, axis)
    parts = [lax.ppermute(x, axis, list(enumerate(step))) for step in steps(n, axis)]
    return call(sum_kernel, shape(*x.shape), vmem(n))(x, *parts)


def shards(features, weight, pair_tiles, pair_count, tile_vals, cotangent):
    rows, width = features.shape
    _, n_own, slots, tile, _ = tile_vals.shape
    col_tiles = rows // tile
    half = rows // 2
    n_rep = lax.axis_size("rep")
    row_tiles = n_rep * col_tiles
    tiles = tile_vals[0]
    live = jnp.arange(slots)[None, :] < pair_count[0][:, None]
    slots_of = jnp.where(live, pair_tiles[0], -1)

    packed = call(
        pack_kernel,
        shape(half, width, dtype=bf16),
        vmem(1),
        cost=pl.CostEstimate(flops=0, bytes_accessed=10**7, transcendentals=0),
    )(features)
    if n_own <= LONGEST:
        blocks = [
            lax.ppermute(packed, "row", list(enumerate(step))) for step in steps(n_own, "gather")
        ]
    else:
        blocks = [lax.all_gather(packed, "row")]
    sources = pltpu.VMEM((col_tiles, tile, width), bf16)
    lists = vmem(2)
    cost = pl.CostEstimate(flops=10**8, bytes_accessed=3 * 10**6, transcendentals=0)
    total_shape = shape(row_tiles + 1, tile, width)
    total, degrees = call(
        own_kernel,
        [total_shape, shape(row_tiles, tile)],
        lists + vmem(1),
        [sources],
        cost,
    )(tiles, slots_of, packed)
    messages = [shape(half + 8, width)] * n_rep
    if n_own <= LONGEST:
        for step, block in zip(steps(n_own, "gather")[:-1], blocks):
            total = call(
                functools.partial(fold_kernel, step),
                total_shape,
                lists + vmem(2),
                [sources],
                cost,
                {3: 0},
            )(tiles, slots_of, block, total)
        mine, *sends = call(
            functools.partial(last_kernel, steps(n_own, "gather")[-1]),
            messages,
            lists + vmem(3),
            [pltpu.VMEM(total_shape.shape, f32), sources],
        )(tiles, slots_of, blocks[-1], total, degrees)
    else:
        total = call(fold_all_kernel, total_shape, lists + vmem(2), [sources], cost, {3: 0})(
            tiles, slots_of, blocks[0], total
        )
        mine, *sends = call(send_kernel, messages, vmem(2))(total, degrees)
    parts = [
        lax.ppermute(sent, "rep", list(enumerate(step)))
        for step, sent in zip(steps(n_rep, "partials"), sends)
    ]
    mine = call(sum_kernel, messages[0], vmem(n_rep))(mine, *parts)
    other = lax.ppermute(mine[:half], "feat", [(0, 1), (1, 0)])
    activated_shape = shape(rows, weight.shape[1], dtype=bf16)
    activated, grad = call(
        layer_kernel,
        [activated_shape, shape(width, weight.shape[1])],
        vmem(5),
    )(mine, other, features, weight, cotangent)
    grad = total_over(grad, "rep")
    grad = total_over(grad, "row")
    activated = call(copy_kernel, activated_shape, vmem(1))(activated)
    return activated, grad


def solution(mesh):
    return jax.shard_map(
        shards,
        mesh=mesh,
        in_specs=(
            P(("row", "rep"), None),
            P(None, "feat"),
            P(("row", "rep"), None, None),
            P(("row", "rep"), None),
            P(("row", "rep"), None, None, None, None),
            P(("row", "rep"), "feat"),
        ),
        out_specs=(P(("row", "rep"), "feat"), P(None, "feat")),
        check_vma=False,
    )
```

```python
import functools

import jax
import jax.numpy as jnp
from jax import lax
from jax.experimental import pallas as pl
from jax.experimental.pallas import tpu as pltpu
from jax.sharding import PartitionSpec as P

f32 = jnp.float32
bf16 = jnp.bfloat16
LONGEST = 8
STEPS = {
    "gather": [(2, 3, 1, 0), (1, 0, 3, 2), (3, 2, 0, 1)],
    "partials": [(3, 2, 1, 0), (1, 3, 0, 2), (2, 0, 3, 1)],
    "rep": [(2, 3, 1, 0), (1, 0, 3, 2), (3, 2, 0, 1)],
    "row": [(2, 3, 1, 0), (1, 0, 3, 2), (3, 2, 0, 1)],
}


def vmem(n):
    return [pl.BlockSpec(memory_space=pltpu.VMEM)] * n


def lower_half(shape):
    lane = lax.broadcasted_iota(jnp.int32, shape, len(shape) - 1)
    return lane < shape[-1] // 2


def pack_kernel(x_ref, out_ref):
    half = x_ref.shape[0] // 2
    width = x_ref.shape[1]
    first = lax.axis_index("feat") == 0
    top = x_ref[:half].astype(f32)
    low = x_ref[half:].astype(f32)
    kept = jnp.where(first, top, low)
    moved = pltpu.roll(jnp.where(first, low, top), width // 2, 1)
    left = lower_half(kept.shape)
    out_ref[...] = jnp.where(left == first, kept, moved).astype(bf16)


def spread(x, sources_ref, tile):
    x = x.astype(f32)
    left = lower_half(x.shape)
    top = jnp.where(left, x, 0.0).astype(bf16)
    low = jnp.where(left, pltpu.roll(x, x.shape[1] // 2, 1), 0.0).astype(bf16)
    n = x.shape[0] // tile
    for c in range(n):
        sources_ref[c] = top[c * tile : (c + 1) * tile]
        sources_ref[n + c] = low[c * tile : (c + 1) * tile]


def add_tiles(j, tiles_ref, list_ref, sources_ref, acc_ref):
    col_tiles = sources_ref.shape[0]
    spare = acc_ref.shape[0] - 1
    listed = list_ref[pl.ds(j, 1)]
    for p in range(tiles_ref.shape[1]):
        t = listed[0, p]
        i = jnp.where(t < 0, spare, t // col_tiles)
        acc_ref[i] += jnp.dot(
            tiles_ref[j, p], sources_ref[jnp.maximum(t, 0) % col_tiles], preferred_element_type=f32
        )


def own_kernel(tiles_ref, list_ref, x_ref, acc_ref, deg_ref, sources_ref):
    n_own, slots, tile, _ = tiles_ref.shape
    col_tiles = sources_ref.shape[0]
    row_tiles = acc_ref.shape[0] - 1
    acc_ref[...] = jnp.zeros_like(acc_ref)
    spread(x_ref[...], sources_ref, tile)
    add_tiles(lax.axis_index("row"), tiles_ref, list_ref, sources_ref, acc_ref)
    lane = lax.broadcasted_iota(jnp.int32, (tile, 128), 1)


    def sums_of(j, total):
        listed = list_ref[pl.ds(j, 1)]
        rows = jnp.where(listed < 0, -1, listed // col_tiles)
        for p in range(slots):
            mark = (lane == rows[:, p : p + 1]).astype(f32).astype(bf16)
            total = total + jnp.dot(tiles_ref[j, p], mark, preferred_element_type=f32)
        return total

    total = jnp.zeros((tile, 128), f32)
    if n_own <= LONGEST:
        for j in range(n_own):
            total = sums_of(j, total)
    else:
        total = lax.fori_loop(0, n_own, sums_of, total)
    deg_ref[...] = total.T[:row_tiles]


def fold_kernel(step, tiles_ref, list_ref, block_ref, start_ref, acc_ref, sources_ref):
    tile = tiles_ref.shape[2]
    spread(block_ref[...], sources_ref, tile)
    j = sender(step, lax.axis_index("row"))
    add_tiles(j, tiles_ref, list_ref, sources_ref, acc_ref)


def fold_all_kernel(tiles_ref, list_ref, blocks_ref, start_ref, acc_ref, sources_ref):
    n_own, _, tile, _ = tiles_ref.shape
    me = lax.axis_index("row")

    @pl.loop(1, n_own)
    def _(k):
        j = lax.rem(me + k, n_own)
        spread(blocks_ref[j], sources_ref, tile)
        add_tiles(j, tiles_ref, list_ref, sources_ref, acc_ref)


def send_kernel(acc_ref, deg_ref, *outs):
    tile, width = acc_ref.shape[1:]
    row_tiles = acc_ref.shape[0] - 1
    rep = lax.axis_index("rep")
    n_rep = len(outs)
    col_tiles = row_tiles // n_rep
    n = col_tiles // 2
    left = lower_half((tile, width))
    for k, out in enumerate(outs):
        q = rep if k == 0 else target(steps(n_rep, "partials")[k - 1], rep)
        for c in range(n):
            top = acc_ref[q * col_tiles + c]
            low = acc_ref[q * col_tiles + n + c]
            out[c * tile : (c + 1) * tile] = jnp.where(left, top, pltpu.roll(low, width // 2, 1))
        rows = out.shape[0] - n * tile
        out[n * tile :] = jnp.zeros((rows, width), f32)
        for c in range(col_tiles):
            out[n * tile + c : n * tile + c + 1] = deg_ref[pl.ds(q * col_tiles + c, 1)]


def last_kernel(step, *refs):
    acc_ref, sources_ref = refs[-2:]
    tiles_ref, list_ref, block_ref, start_ref, deg_ref = refs[:5]
    acc_ref[...] = start_ref[...]
    spread(block_ref[...], sources_ref, tiles_ref.shape[2])
    j = sender(step, lax.axis_index("row"))
    add_tiles(j, tiles_ref, list_ref, sources_ref, acc_ref)
    send_kernel(acc_ref, deg_ref, *refs[5:-2])


def copy_kernel(x_ref, out_ref):
    out_ref[...] = x_ref[...]


def sum_kernel(*refs):
    total = refs[0][...]
    for ref in refs[1:-1]:
        total = total + ref[...]
    refs[-1][...] = total


def split(x):
    high = x.astype(bf16)
    return high, (x - high.astype(f32)).astype(bf16)


def layer_kernel(mine_ref, other_ref, x_ref, w_ref, cot_ref, act_ref, grad_ref):
    half = other_ref.shape[0]
    width = other_ref.shape[1]
    tile = 128
    first = lax.axis_index("feat") == 0
    mine = mine_ref[:half]
    other = other_ref[...]
    here = jnp.where(first, mine, other)
    there = jnp.where(first, other, mine)
    left = lower_half(here.shape)
    top = jnp.where(left, here, pltpu.roll(there, width // 2, 1)) + x_ref[:half].astype(f32)
    low = jnp.where(left, pltpu.roll(here, width // 2, 1), there) + x_ref[half:].astype(f32)
    agg = jnp.concatenate([top, low], axis=0)
    scales = lax.rsqrt(mine_ref[half:] + 1.0)
    rows = scales.shape[0]
    turned = jnp.concatenate([scales] * (128 // rows), axis=0).T
    scale = jnp.concatenate(
        [jnp.broadcast_to(turned[:, c : c + 1], (tile, 128)) for c in range(2 * half // tile)],
        axis=0,
    )
    both = jnp.concatenate(split(agg), axis=1)
    w = w_ref[...]
    preact = scale * jnp.dot(both, jnp.concatenate([w, w], axis=0), preferred_element_type=f32)
    sig = 1.0 / (1.0 + jnp.exp(-preact))
    act_ref[...] = (preact * sig).astype(bf16)
    slopes = scale * cot_ref[...].astype(f32) * sig * (1.0 + preact * (1.0 - sig))
    width = agg.shape[1]
    hidden = slopes.shape[1]
    terms = lax.dot_general(
        both,
        jnp.concatenate(split(slopes), axis=1),
        (((0,), (0,)), ((), ())),
        preferred_element_type=f32,
    )
    grad_ref[...] = (
        terms[:width, :hidden] + terms[:width, hidden:] + terms[width:, :hidden]
        + terms[width:, hidden:]
    )


def shape(*dims, dtype=f32):
    return jax.ShapeDtypeStruct(dims, dtype)


def call(kernel, outs, in_specs, scratch=(), cost=None, aliases=None):
    return pl.pallas_call(
        kernel,
        out_shape=outs,
        in_specs=in_specs,
        out_specs=vmem(1)[0] if not isinstance(outs, (list, tuple)) else vmem(len(outs)),
        scratch_shapes=list(scratch),
        compiler_params=pltpu.CompilerParams(vmem_limit_bytes=48 * 1024 * 1024),
        cost_estimate=cost,
        input_output_aliases=aliases or {},
    )


def steps(n, phase):
    if n == 4:
        return STEPS[phase]
    return [tuple(i ^ k for i in range(n)) for k in range(n - 1, 0, -1)]


def target(step, me):
    j = jnp.int32(0)
    for i, to in enumerate(step):
        j = jnp.where(me == i, to, j)
    return j


def sender(step, me):
    j = jnp.int32(0)
    for i, target in enumerate(step):
        j = jnp.where(me == target, i, j)
    return j


def total_over(x, axis):
    n = lax.axis_size(axis)
    if n > LONGEST:
        return lax.psum(x, axis)
    parts = [lax.ppermute(x, axis, list(enumerate(step))) for step in steps(n, axis)]
    return call(sum_kernel, shape(*x.shape), vmem(n))(x, *parts)


def shards(features, weight, pair_tiles, pair_count, tile_vals, cotangent):
    rows, width = features.shape
    _, n_own, slots, tile, _ = tile_vals.shape
    col_tiles = rows // tile
    half = rows // 2
    n_rep = lax.axis_size("rep")
    row_tiles = n_rep * col_tiles
    tiles = tile_vals[0]
    live = jnp.arange(slots)[None, :] < pair_count[0][:, None]
    slots_of = jnp.where(live, pair_tiles[0], -1)

    packed = call(
        pack_kernel,
        shape(half, width, dtype=bf16),
        vmem(1),
        cost=pl.CostEstimate(flops=0, bytes_accessed=10**7, transcendentals=0),
    )(features)
    if n_own <= LONGEST:
        blocks = [
            lax.ppermute(packed, "row", list(enumerate(step))) for step in steps(n_own, "gather")
        ]
    else:
        blocks = [lax.all_gather(packed, "row")]
    sources = pltpu.VMEM((col_tiles, tile, width), bf16)
    lists = vmem(2)
    cost = pl.CostEstimate(flops=10**8, bytes_accessed=3 * 10**6, transcendentals=0)
    total_shape = shape(row_tiles + 1, tile, width)
    total, degrees = call(
        own_kernel,
        [total_shape, shape(row_tiles, tile)],
        lists + vmem(1),
        [sources],
        cost,
    )(tiles, slots_of, packed)
    messages = [shape(half + 8, width)] * n_rep
    if n_own <= LONGEST:
        for step, block in zip(steps(n_own, "gather")[:-1], blocks):
            total = call(
                functools.partial(fold_kernel, step),
                total_shape,
                lists + vmem(2),
                [sources],
                cost,
                {3: 0},
            )(tiles, slots_of, block, total)
        mine, *sends = call(
            functools.partial(last_kernel, steps(n_own, "gather")[-1]),
            messages,
            lists + vmem(3),
            [pltpu.VMEM(total_shape.shape, f32), sources],
        )(tiles, slots_of, blocks[-1], total, degrees)
    else:
        total = call(fold_all_kernel, total_shape, lists + vmem(2), [sources], cost, {3: 0})(
            tiles, slots_of, blocks[0], total
        )
        mine, *sends = call(send_kernel, messages, vmem(2))(total, degrees)
    parts = [
        lax.ppermute(sent, "rep", list(enumerate(step)))
        for step, sent in zip(steps(n_rep, "partials"), sends)
    ]
    mine = call(sum_kernel, messages[0], vmem(n_rep))(mine, *parts)
    other = lax.ppermute(mine[:half], "feat", [(0, 1), (1, 0)])
    activated_shape = shape(rows, weight.shape[1], dtype=bf16)
    activated, grad = call(
        layer_kernel,
        [activated_shape, shape(width, weight.shape[1])],
        vmem(5),
    )(mine, other, features, weight, cotangent)
    grad = total_over(grad, "rep")
    grad = total_over(grad, "row")
    activated = call(copy_kernel, activated_shape, vmem(1))(activated)
    return activated, grad


def solution(mesh):
    return jax.shard_map(
        shards,
        mesh=mesh,
        in_specs=(
            P(("row", "rep"), None),
            P(None, "feat"),
            P(("row", "rep"), None, None),
            P(("row", "rep"), None),
            P(("row", "rep"), None, None, None, None),
            P(("row", "rep"), "feat"),
        ),
        out_specs=(P(("row", "rep"), "feat"), P(None, "feat")),
        check_vma=False,
    )
```

```python
import functools

import jax
import jax.numpy as jnp
from jax import lax
from jax.experimental import pallas as pl
from jax.experimental.pallas import tpu as pltpu
from jax.sharding import PartitionSpec as P

f32 = jnp.float32
bf16 = jnp.bfloat16
LONGEST = 8
STEPS = {
    "gather": [(2, 3, 1, 0), (1, 0, 3, 2), (3, 2, 0, 1)],
    "partials": [(3, 2, 1, 0), (1, 3, 0, 2), (2, 0, 3, 1)],
    "rep": [(2, 3, 1, 0), (1, 0, 3, 2), (3, 2, 0, 1)],
    "row": [(2, 3, 1, 0), (1, 0, 3, 2), (3, 2, 0, 1)],
}


def vmem(n):
    return [pl.BlockSpec(memory_space=pltpu.VMEM)] * n


def lower_half(shape):
    lane = lax.broadcasted_iota(jnp.int32, shape, len(shape) - 1)
    return lane < shape[-1] // 2


def pack_kernel(x_ref, out_ref):
    half = x_ref.shape[0] // 2
    width = x_ref.shape[1]
    first = lax.axis_index("feat") == 0
    top = x_ref[:half].astype(f32)
    low = x_ref[half:].astype(f32)
    kept = jnp.where(first, top, low)
    moved = pltpu.roll(jnp.where(first, low, top), width // 2, 1)
    left = lower_half(kept.shape)
    out_ref[...] = jnp.where(left == first, kept, moved).astype(bf16)


def spread(x, sources_ref, tile):
    x = x.astype(f32)
    left = lower_half(x.shape)
    top = jnp.where(left, x, 0.0).astype(bf16)
    low = jnp.where(left, pltpu.roll(x, x.shape[1] // 2, 1), 0.0).astype(bf16)
    n = x.shape[0] // tile
    for c in range(n):
        sources_ref[c] = top[c * tile : (c + 1) * tile]
        sources_ref[n + c] = low[c * tile : (c + 1) * tile]


def add_tiles(j, tiles_ref, list_ref, sources_ref, acc_ref):
    col_tiles = sources_ref.shape[0]
    spare = acc_ref.shape[0] - 1
    listed = list_ref[pl.ds(j, 1)]
    for p in range(tiles_ref.shape[1]):
        t = listed[0, p]
        i = jnp.where(t < 0, spare, t // col_tiles)
        acc_ref[i] += jnp.dot(
            tiles_ref[j, p], sources_ref[jnp.maximum(t, 0) % col_tiles], preferred_element_type=f32
        )


def own_kernel(tiles_ref, list_ref, x_ref, acc_ref, deg_ref, sources_ref):
    n_own, slots, tile, _ = tiles_ref.shape
    col_tiles = sources_ref.shape[0]
    row_tiles = acc_ref.shape[0] - 1
    acc_ref[...] = jnp.zeros_like(acc_ref)
    spread(x_ref[...], sources_ref, tile)
    add_tiles(lax.axis_index("row"), tiles_ref, list_ref, sources_ref, acc_ref)
    lane = lax.broadcasted_iota(jnp.int32, (tile, 128), 1)


    def sums_of(j, total):
        listed = list_ref[pl.ds(j, 1)]
        rows = jnp.where(listed < 0, -1, listed // col_tiles)
        for p in range(slots):
            mark = (lane == rows[:, p : p + 1]).astype(f32).astype(bf16)
            total = total + jnp.dot(tiles_ref[j, p], mark, preferred_element_type=f32)
        return total

    total = jnp.zeros((tile, 128), f32)
    if n_own <= LONGEST:
        for j in range(n_own):
            total = sums_of(j, total)
    else:
        total = lax.fori_loop(0, n_own, sums_of, total)
    deg_ref[...] = total.T[:row_tiles]


def fold_kernel(step, tiles_ref, list_ref, block_ref, start_ref, acc_ref, sources_ref):
    tile = tiles_ref.shape[2]
    spread(block_ref[...], sources_ref, tile)
    j = sender(step, lax.axis_index("row"))
    add_tiles(j, tiles_ref, list_ref, sources_ref, acc_ref)


def fold_all_kernel(tiles_ref, list_ref, blocks_ref, start_ref, acc_ref, sources_ref):
    n_own, _, tile, _ = tiles_ref.shape
    me = lax.axis_index("row")

    @pl.loop(1, n_own)
    def _(k):
        j = lax.rem(me + k, n_own)
        spread(blocks_ref[j], sources_ref, tile)
        add_tiles(j, tiles_ref, list_ref, sources_ref, acc_ref)


def send_kernel(acc_ref, deg_ref, *outs):
    tile, width = acc_ref.shape[1:]
    row_tiles = acc_ref.shape[0] - 1
    rep = lax.axis_index("rep")
    n_rep = len(outs)
    col_tiles = row_tiles // n_rep
    n = col_tiles // 2
    left = lower_half((tile, width))
    for k, out in enumerate(outs):
        q = rep if k == 0 else target(steps(n_rep, "partials")[k - 1], rep)
        for c in range(n):
            top = acc_ref[q * col_tiles + c]
            low = acc_ref[q * col_tiles + n + c]
            out[c * tile : (c + 1) * tile] = jnp.where(left, top, pltpu.roll(low, width // 2, 1))
        rows = out.shape[0] - n * tile
        out[n * tile :] = jnp.zeros((rows, width), f32)
        for c in range(col_tiles):
            out[n * tile + c : n * tile + c + 1] = deg_ref[pl.ds(q * col_tiles + c, 1)]


def last_kernel(step, *refs):
    acc_ref, sources_ref = refs[-2:]
    tiles_ref, list_ref, block_ref, start_ref, deg_ref = refs[:5]
    acc_ref[...] = start_ref[...]
    spread(block_ref[...], sources_ref, tiles_ref.shape[2])
    j = sender(step, lax.axis_index("row"))
    add_tiles(j, tiles_ref, list_ref, sources_ref, acc_ref)
    send_kernel(acc_ref, deg_ref, *refs[5:-2])


def copy_kernel(x_ref, out_ref):
    out_ref[...] = x_ref[...]


def sum_kernel(*refs):
    total = refs[0][...]
    for ref in refs[1:-1]:
        total = total + ref[...]
    refs[-1][...] = total


def split(x):
    high = x.astype(bf16)
    return high, (x - high.astype(f32)).astype(bf16)


def unpack(x, core):
    width = x.shape[1]
    moved = pltpu.roll(x, width // 2, 1)
    first = core == 0
    here = lower_half(x.shape) == first
    top = jnp.where(here, jnp.where(first, x, moved), 0.0)
    low = jnp.where(here, jnp.where(first, moved, x), 0.0)
    return jnp.concatenate([top, low], axis=0)


def before_kernel(mine_ref, x_ref, w_ref, agg_ref, scale_ref, preact_ref):
    half = x_ref.shape[0] // 2
    tile = 128
    agg = unpack(mine_ref[:half], lax.axis_index("feat")) + x_ref[...].astype(f32)
    agg_ref[...] = agg
    scales = lax.rsqrt(mine_ref[half:] + 1.0)
    turned = jnp.concatenate([scales] * (128 // scales.shape[0]), axis=0).T
    for c in range(2 * half // tile):
        scale_ref[c * tile : (c + 1) * tile] = jnp.broadcast_to(turned[:, c : c + 1], (tile, 128))
    both = jnp.concatenate(split(agg), axis=1)
    w = w_ref[...]
    preact_ref[...] = jnp.dot(both, jnp.concatenate([w, w], axis=0), preferred_element_type=f32)


def layer_kernel(
    other_ref, agg_ref, scale_ref, preact_ref, w_ref, cot_ref, act_ref, grad_ref
):
    other = unpack(other_ref[...], 1 - lax.axis_index("feat"))
    w = w_ref[...]
    both = jnp.concatenate(split(other), axis=1)
    preact = scale_ref[...] * (
        preact_ref[...]
        + jnp.dot(both, jnp.concatenate([w, w], axis=0), preferred_element_type=f32)
    )
    scale = scale_ref[...]
    agg = agg_ref[...] + other
    both = jnp.concatenate(split(agg), axis=1)
    sig = 1.0 / (1.0 + jnp.exp(-preact))
    act_ref[...] = (preact * sig).astype(bf16)
    slopes = scale * cot_ref[...].astype(f32) * sig * (1.0 + preact * (1.0 - sig))
    width = agg.shape[1]
    hidden = slopes.shape[1]
    terms = lax.dot_general(
        both,
        jnp.concatenate(split(slopes), axis=1),
        (((0,), (0,)), ((), ())),
        preferred_element_type=f32,
    )
    grad_ref[...] = (
        terms[:width, :hidden] + terms[:width, hidden:] + terms[width:, :hidden]
        + terms[width:, hidden:]
    )


def shape(*dims, dtype=f32):
    return jax.ShapeDtypeStruct(dims, dtype)


def call(kernel, outs, in_specs, scratch=(), cost=None, aliases=None):
    return pl.pallas_call(
        kernel,
        out_shape=outs,
        in_specs=in_specs,
        out_specs=vmem(1)[0] if not isinstance(outs, (list, tuple)) else vmem(len(outs)),
        scratch_shapes=list(scratch),
        compiler_params=pltpu.CompilerParams(vmem_limit_bytes=48 * 1024 * 1024),
        cost_estimate=cost,
        input_output_aliases=aliases or {},
    )


def steps(n, phase):
    if n == 4:
        return STEPS[phase]
    return [tuple(i ^ k for i in range(n)) for k in range(n - 1, 0, -1)]


def target(step, me):
    j = jnp.int32(0)
    for i, to in enumerate(step):
        j = jnp.where(me == i, to, j)
    return j


def sender(step, me):
    j = jnp.int32(0)
    for i, target in enumerate(step):
        j = jnp.where(me == target, i, j)
    return j


def total_over(x, axis):
    n = lax.axis_size(axis)
    if n > LONGEST:
        return lax.psum(x, axis)
    parts = [lax.ppermute(x, axis, list(enumerate(step))) for step in steps(n, axis)]
    return call(sum_kernel, shape(*x.shape), vmem(n))(x, *parts)


def shards(features, weight, pair_tiles, pair_count, tile_vals, cotangent):
    rows, width = features.shape
    _, n_own, slots, tile, _ = tile_vals.shape
    col_tiles = rows // tile
    half = rows // 2
    n_rep = lax.axis_size("rep")
    row_tiles = n_rep * col_tiles
    tiles = tile_vals[0]
    live = jnp.arange(slots)[None, :] < pair_count[0][:, None]
    slots_of = jnp.where(live, pair_tiles[0], -1)

    packed = call(
        pack_kernel,
        shape(half, width, dtype=bf16),
        vmem(1),
        cost=pl.CostEstimate(flops=0, bytes_accessed=10**7, transcendentals=0),
    )(features)
    if n_own <= LONGEST:
        blocks = [
            lax.ppermute(packed, "row", list(enumerate(step))) for step in steps(n_own, "gather")
        ]
    else:
        blocks = [lax.all_gather(packed, "row")]
    sources = pltpu.VMEM((col_tiles, tile, width), bf16)
    lists = vmem(2)
    cost = pl.CostEstimate(flops=10**8, bytes_accessed=3 * 10**6, transcendentals=0)
    total_shape = shape(row_tiles + 1, tile, width)
    total, degrees = call(
        own_kernel,
        [total_shape, shape(row_tiles, tile)],
        lists + vmem(1),
        [sources],
        cost,
    )(tiles, slots_of, packed)
    messages = [shape(half + 8, width)] * n_rep
    if n_own <= LONGEST:
        for step, block in zip(steps(n_own, "gather")[:-1], blocks):
            total = call(
                functools.partial(fold_kernel, step),
                total_shape,
                lists + vmem(2),
                [sources],
                cost,
                {3: 0},
            )(tiles, slots_of, block, total)
        mine, *sends = call(
            functools.partial(last_kernel, steps(n_own, "gather")[-1]),
            messages,
            lists + vmem(3),
            [pltpu.VMEM(total_shape.shape, f32), sources],
        )(tiles, slots_of, blocks[-1], total, degrees)
    else:
        total = call(fold_all_kernel, total_shape, lists + vmem(2), [sources], cost, {3: 0})(
            tiles, slots_of, blocks[0], total
        )
        mine, *sends = call(send_kernel, messages, vmem(2))(total, degrees)
    parts = [
        lax.ppermute(sent, "rep", list(enumerate(step)))
        for step, sent in zip(steps(n_rep, "partials"), sends)
    ]
    mine = call(sum_kernel, messages[0], vmem(n_rep))(mine, *parts)
    other = lax.ppermute(mine[:half], "feat", [(0, 1), (1, 0)])
    activated_shape = shape(rows, weight.shape[1], dtype=bf16)
    agg, scale, preact = call(
        before_kernel,
        [shape(rows, width), shape(rows, width), shape(rows, weight.shape[1])],
        vmem(3),
        cost=pl.CostEstimate(flops=10**8, bytes_accessed=3 * 10**6, transcendentals=0),
    )(mine, features, weight)
    activated, grad = call(
        layer_kernel,
        [activated_shape, shape(width, weight.shape[1])],
        vmem(6),
    )(other, agg, scale, preact, weight, cotangent)
    grad = total_over(grad, "rep")
    grad = total_over(grad, "row")
    activated = call(copy_kernel, activated_shape, vmem(1))(activated)
    return activated, grad


def solution(mesh):
    return jax.shard_map(
        shards,
        mesh=mesh,
        in_specs=(
            P(("row", "rep"), None),
            P(None, "feat"),
            P(("row", "rep"), None, None),
            P(("row", "rep"), None),
            P(("row", "rep"), None, None, None, None),
            P(("row", "rep"), "feat"),
        ),
        out_specs=(P(("row", "rep"), "feat"), P(None, "feat")),
        check_vma=False,
    )
```
